32 devices in a mesh: shard: 8 (over y, x, core), ctx: 4 (over z).
Axes of the slice: x: 2, y: 2, z: 4, core: 2. Of those that a mesh axis runs over, the one named last changes fastest.
Arguments:
- embedded: bfloat16 [4096, 8192], P('shard', 'ctx'), may hold values from -6 to 6
- w_query: bfloat16 [8192, 4096], P('shard', 'ctx'), may hold values from -0.0625 to 0.0625
- w_key: bfloat16 [8192, 4096], P('shard', 'ctx'), may hold values from -0.0625 to 0.0625
- w_value: bfloat16 [8192, 4096], P('shard', 'ctx'), may hold values from -0.0625 to 0.0625
- short_taps: float32 [3, 3, 4096], P(None, None, 'ctx'), may hold values from -3 to 3
- long_filter: float32 [128, 256], P(None, 'ctx'), may hold values from -0.5 to 0.5
- skip_gain: float32 [4096], P('ctx'), may hold values from -4 to 4
Outputs:
- gated: bfloat16 [4096, 4096], P('shard', 'ctx')
The draws below stay inside these ranges and needn't reach their ends.
All inputs are finite; a program needn't handle non-finite values.
Results may differ from the reference program's by a relative error of at most 0.007.
Values may be sent and summed in bfloat16 or wider, within the bound.
A program may use at most 128 MiB of HBM per device.

```python
import jax
import jax.numpy as jnp
from jax import lax

D = 8192
C = 4096
GROUP = 16
TAPS = 128
FILTERS = 256
LENGTH = 4096


def block_scale(stream_key, dims, shards, least, largest):
    def one(position, parts):
        heights = jax.random.uniform(jax.random.fold_in(jax.random.fold_in(stream_key, 6), position), (parts,), jnp.float32, least / len(shards), largest / len(shards))
        return jnp.repeat(jnp.exp(heights), dims[position] // parts).reshape((-1,) + (1,) * (len(dims) - position - 1))

    factor_of = one(*shards[0])
    for cut in shards[1:]:
        factor_of = factor_of * one(*cut)
    return factor_of


def centred(own_key, dims, spread, most, shards=(), kind=jnp.bfloat16):
    array = spread * jax.random.normal(own_key, dims, jnp.float32)
    if shards:
        array = array * block_scale(own_key, dims, shards, -0.22, 0.18)
    return jnp.clip(array, -most, most).astype(kind)


def setup_inputs(seed: int = 0) -> dict:
    keys = jax.random.split(jax.random.key(seed), 8)
    embedded = centred(keys[0], (LENGTH, D), 1.0, 6.0, ((0, 8), (1, 4)))
    w_query = centred(keys[1], (D, C), D ** -0.5, 0.0625, ((0, 8), (1, 4)))
    w_key = centred(keys[2], (D, C), D ** -0.5, 0.0625, ((0, 8), (1, 4)))
    w_value = centred(keys[3], (D, C), D ** -0.5, 0.0625, ((0, 8), (1, 4)))
    short_taps = centred(keys[4], (3, 3, C), 0.6, 3.0, ((2, 4),), jnp.float32)
    long_filter = centred(keys[5], (TAPS, FILTERS), 0.09, 0.5, ((1, 4),), jnp.float32)
    skip_gain = centred(keys[6], (C,), 1.0, 4.0, ((0, 4),), jnp.float32)
    return {"embedded": embedded, "w_query": w_query, "w_key": w_key, "w_value": w_value, "short_taps": short_taps, "long_filter": long_filter, "skip_gain": skip_gain}


def short_conv(field_rows, tap_weights):
    values = field_rows.astype(jnp.float32)
    shifted_one = jnp.pad(values, ((1, 0), (0, 0)))[:-1]
    shifted_two = jnp.pad(values, ((2, 0), (0, 0)))[:-2]
    return tap_weights[0] * values + tap_weights[1] * shifted_one + tap_weights[2] * shifted_two


def reference(embedded, w_query, w_key, w_value, short_taps, long_filter, skip_gain):
    query_rows = jnp.dot(embedded, w_query, preferred_element_type=jnp.float32).astype(jnp.bfloat16)
    key_rows = jnp.dot(embedded, w_key, preferred_element_type=jnp.float32).astype(jnp.bfloat16)
    value_rows = jnp.dot(embedded, w_value, preferred_element_type=jnp.float32).astype(jnp.bfloat16)
    query_short = short_conv(query_rows, short_taps[0])
    key_short = short_conv(key_rows, short_taps[1])
    value_short = short_conv(value_rows, short_taps[2])
    mixed_rows = (key_short * value_short).astype(jnp.bfloat16)
    seq_length = mixed_rows.shape[0]
    padded = jnp.concatenate([jnp.zeros((TAPS - 1, C), jnp.float32), mixed_rows.astype(jnp.float32)], axis=0)
    channel_taps = jnp.repeat(long_filter, GROUP, axis=1)

    def add_tap(tap_index, running):
        lag_index = jnp.asarray(tap_index).astype(jnp.int32)
        begin_row = (TAPS - 1 - lag_index).astype(jnp.int32)
        window = lax.dynamic_slice_in_dim(padded, begin_row, seq_length, 0)
        tap_row = lax.dynamic_index_in_dim(channel_taps, lag_index, 0, keepdims=False)
        return running + tap_row * window

    long_out = lax.fori_loop(0, TAPS, add_tap, jnp.zeros((seq_length, C), jnp.float32))
    return (query_short * (long_out + skip_gain * mixed_rows.astype(jnp.float32))).astype(jnp.bfloat16)
```

```python
import functools

import jax
import jax.numpy as jnp
from jax import lax
from jax.experimental import pallas as pl
from jax.experimental.pallas import tpu as pltpu
from jax.sharding import PartitionSpec as P

CHUNKS = 4
HALVES = 2
PIECES = 4
AHEAD = 2
TILE = 256
MESH = pl.DeviceIdType.MESH


def forward(value, axis, steps):
    count = lax.axis_size(axis)
    return lax.ppermute(value, axis, [(source, source + steps) for source in range(count - steps)])


def projection_kernel(
    names, embedded, w_key, w_value, w_query, out,
    wbuf, ebuf, gbuf, osend, orecv, acc,
    wy_sem, wc_sem, wo_sem, zs_sem, zr_sem, x_sem, o_sem, local_sem,
):
    shards, blocks = lax.axis_size(names[0]), lax.axis_size(names[1])
    per = shards // blocks
    groups = blocks // 2
    place, z = lax.axis_index(names[0]), lax.axis_index(names[1])
    core = place % per
    side = (place // per) % 2
    group = place // (2 * per)
    weights = (w_key, w_value, w_query)
    rows, wide = embedded.shape
    depth, width = w_key.shape
    piece = rows // CHUNKS
    half = rows // HALVES
    cut = depth // PIECES
    core_place = place + 1 - 2 * core
    side_place = place + per * (1 - 2 * side)

    def group_place(step):
        return lax.rem(group + step, groups) * 2 * per + side * per + core

    def remote(src, dst, send, recv, where):
        return pltpu.make_async_remote_copy(
            src_ref=src, dst_ref=dst, send_sem=send, recv_sem=recv,
            device_id=where, device_id_type=MESH,
        )

    def either(body, *conditions):
        flag = conditions[0]
        for other in conditions[1:]:
            flag = jnp.logical_and(flag, other)
        pl.when(flag)(body)

    barrier = pltpu.get_barrier_semaphore()
    partners = [core_place, side_place] + [group_place(j) for j in range(1, groups)]
    for partner in partners:
        pl.semaphore_signal(barrier, inc=1, device_id=(partner, z), device_id_type=MESH)

    @pl.when(z > 0)
    def _():
        pl.semaphore_signal(barrier, inc=1, device_id=(place, z - 1), device_id_type=MESH)

    @pl.when(z < blocks - 1)
    def _():
        pl.semaphore_signal(barrier, inc=1, device_id=(place, z + 1), device_id_type=MESH)

    ends = jnp.where(z > 0, 1, 0) + jnp.where(z < blocks - 1, 1, 0)
    pl.semaphore_wait(barrier, len(partners) + ends)

    def chunk(c):
        return pl.ds(c * piece, piece)

    def own_rows(k):
        return pl.ds(pl.multiple_of(core * depth + k * cut, 16), cut)

    pieces = [(p, j, k) for p in range(3) for j in range(1, groups) for k in range(PIECES)]

    def w_across(q):
        p, j, k = pieces[q]
        return remote(
            weights[p].at[pl.ds(k * cut, cut)], wbuf.at[p, j, own_rows(k)],
            wy_sem.at[0, q], wy_sem.at[1, q], (group_place(groups - j), z),
        )

    def w_core(q):
        p, j, k = pieces[q]
        ref = wbuf.at[p, j, own_rows(k)]
        return remote(ref, ref, wc_sem.at[0, q], wc_sem.at[1, q], (core_place, z))

    def w_own(p):
        mine = pl.ds(pl.multiple_of(core * depth, 16), depth)
        return remote(
            weights[p], wbuf.at[p, 0, mine], wo_sem.at[0, p], wo_sem.at[1, p], (core_place, z)
        )

    def w_here(p):
        mine = pl.ds(pl.multiple_of(core * depth, 16), depth)
        return pltpu.make_async_copy(weights[p], wbuf.at[p, 0, mine], local_sem.at[p])

    def up(c, r):
        src = embedded.at[chunk(c)] if r == 1 else ebuf.at[z - (r - 1), chunk(c)]
        return remote(
            src, ebuf.at[z - (r - 1), chunk(c)], zs_sem.at[0, c, r - 1], zr_sem.at[0, c, r - 1],
            (place, z + 1),
        )

    def down(c, r):
        src = embedded.at[chunk(c)] if r == 1 else ebuf.at[z + (r - 1), chunk(c)]
        return remote(
            src, ebuf.at[z + (r - 1), chunk(c)], zs_sem.at[1, c, r - 1], zr_sem.at[1, c, r - 1],
            (place, z - 1),
        )

    def across(c, f, src):
        return remote(
            src, gbuf.at[f // 2, chunk(c)], x_sem.at[0, c, f // 2], x_sem.at[1, c, f // 2],
            (side_place, z),
        )

    def own_embedded(c):
        either(lambda: up(c, 1).start(), z < blocks - 1)
        either(lambda: down(c, 1).start(), z > 0)
        either(lambda: across(c, z, embedded.at[chunk(c)]).start(), z % 2 != side)

    def step(c, r):
        @pl.when(z >= r)
        def _():
            f = z - r
            pltpu.make_async_copy(
                ebuf.at[f, chunk(c)], ebuf.at[f, chunk(c)], zr_sem.at[0, c, r - 1]
            ).wait()
            if r < blocks - 1:
                either(lambda: up(c, r + 1).start(), z < blocks - 1)
            either(lambda: across(c, f, ebuf.at[f, chunk(c)]).start(), f % 2 != side)

        @pl.when(z + r < blocks)
        def _():
            f = z + r
            pltpu.make_async_copy(
                ebuf.at[f, chunk(c)], ebuf.at[f, chunk(c)], zr_sem.at[1, c, r - 1]
            ).wait()
            if r < blocks - 1:
                either(lambda: down(c, r + 1).start(), z > 0)
            either(lambda: across(c, f, ebuf.at[f, chunk(c)]).start(), f % 2 != side)

    def product(p, h, lhs, store):
        at = pl.ds(h * half, half)

        def tile(n, carry):
            cols = pl.ds(pl.multiple_of(n * TILE, TILE), TILE)
            total = None
            for j in range(groups):
                term = jnp.dot(
                    lhs(j)[at, :], wbuf[p, j, :, cols], preferred_element_type=jnp.float32
                )
                total = term if total is None else total + term
            store(at, cols, total)
            return carry

        lax.fori_loop(0, width // TILE, tile, 0)

    def o_copy(p, h):
        at = pl.ds(h * half, half)
        return remote(
            osend.at[p, at], orecv.at[p, at], o_sem.at[0, p, h], o_sem.at[1, p, h], (side_place, z)
        )

    def give(p, h):
        def store(at, cols, total):
            osend[p, at, cols] = total.astype(jnp.bfloat16)

        product(p, h, lambda j: gbuf.at[lax.rem(group + j, groups)], store)
        o_copy(p, h).start()

    def keep(p, h):
        def store(at, cols, total):
            acc[p, at, cols] = total

        product(p, h, lambda j: ebuf.at[2 * lax.rem(group + j, groups) + side], store)

    def finish(p, h):
        at = pl.ds(h * half, half)
        o_copy(p, h).wait_recv()
        out[p, at, :] = (acc[p, at, :] + orecv[p, at, :].astype(jnp.float32)).astype(jnp.bfloat16)

    here = pltpu.make_async_copy(embedded, ebuf.at[z], local_sem.at[3])
    own_embedded(0)
    for q in range(min(AHEAD, len(pieces))):
        w_across(q).start()
    own_embedded(1)
    here.start()
    for p in range(3):
        w_here(p).start()
        w_own(p).start()
    here.wait()
    for p in range(3):
        w_here(p).wait()

    steps = CHUNKS * (blocks - 1)
    weight_ready, rows_ready = {}, {}
    done_pieces = 0
    waited_rows, waited_weights, finished = set(), set(), set()
    pending = [(p, h) for h in range(HALVES) for p in range(3)]
    kept = []

    def ready_rows(h):
        if h in waited_rows:
            return
        waited_rows.add(h)
        for c in range(h * CHUNKS // HALVES, (h + 1) * CHUNKS // HALVES):
            for g in range(groups):
                pltpu.make_async_copy(
                    gbuf.at[g, chunk(c)], gbuf.at[g, chunk(c)], x_sem.at[1, c, g]
                ).wait()

    def ready_weight(p):
        if p in waited_weights:
            return
        waited_weights.add(p)
        w_own(p).wait_recv()
        for q, (owner, _, _) in enumerate(pieces):
            if owner == p:
                w_core(q).wait_recv()

    t = 0
    for c in range(CHUNKS):
        for r in range(1, blocks):
            step(c, r)
            if r == 1 and c + 2 < CHUNKS:
                own_embedded(c + 2)
            while done_pieces < (t + 1) * len(pieces) // steps:
                w_across(done_pieces).wait_recv()
                w_core(done_pieces).start()
                if done_pieces + AHEAD < len(pieces):
                    w_across(done_pieces + AHEAD).start()
                done_pieces += 1
            chunks_in = c if r < blocks - 1 else c + 1
            last = t == steps - 1
            whole = [
                p for p in range(3)
                if done_pieces - (0 if last else 1) >= (p + 1) * (len(pieces) // 3)
            ]
            now = [
                (p, h) for p, h in pending
                if p in whole and (h + 1) * CHUNKS // HALVES <= (chunks_in if last else c)
            ]
            for p, h in now:
                pending.remove((p, h))
                ready_rows(h)
                ready_weight(p)
                give(p, h)
                if last:
                    kept.append((p, h))
                else:
                    keep(p, h)
            t += 1
    for p, h in kept:
        keep(p, h)
    for h in range(HALVES):
        for p in range(3):
            finish(p, h)

    for q in range(len(pieces)):
        w_across(q).wait_send()
        w_core(q).wait_send()
    for p in range(3):
        w_own(p).wait_send()
        for h in range(HALVES):
            o_copy(p, h).wait_send()
    for c in range(CHUNKS):
        for g in range(groups):
            pltpu.make_async_copy(
                gbuf.at[g, chunk(c)], gbuf.at[g, chunk(c)], x_sem.at[0, c, g]
            ).wait()
        for r in range(1, blocks):
            either(lambda: up(c, r).wait_send(), z < blocks - 1, z >= r - 1)
            either(lambda: down(c, r).wait_send(), z > 0, z + r - 1 < blocks)


def project(embedded, w_key, w_value, w_query):
    shards, blocks = lax.axis_size("shard"), lax.axis_size("ctx")
    groups = blocks // 2
    rows, wide = embedded.shape
    depth, width = w_key.shape
    pieces = 3 * (groups - 1) * PIECES
    bf16 = jnp.bfloat16
    dma = pltpu.SemaphoreType.DMA
    flops = 2 * 2 * rows * groups * wide * width * 3
    return pl.pallas_call(
        functools.partial(projection_kernel, ("shard", "ctx")),
        out_shape=jax.ShapeDtypeStruct((3, rows, width), bf16),
        in_specs=[pl.BlockSpec(memory_space=pl.ANY)] * 4,
        out_specs=pl.BlockSpec(memory_space=pltpu.VMEM),
        scratch_shapes=[
            pltpu.VMEM((3, groups, wide, width), bf16),
            pltpu.VMEM((blocks, rows, wide), bf16),
            pltpu.VMEM((groups, rows, wide), bf16),
            pltpu.VMEM((3, rows, width), bf16),
            pltpu.VMEM((3, rows, width), bf16),
            pltpu.VMEM((3, rows, width), jnp.float32),
            dma((2, pieces)),
            dma((2, pieces)),
            dma((2, 3)),
            dma((2, CHUNKS, blocks - 1)),
            dma((2, CHUNKS, blocks - 1)),
            dma((2, CHUNKS, groups)),
            dma((2, 3, HALVES)),
            dma((4,)),
        ],
        compiler_params=pltpu.CompilerParams(
            collective_id=0, has_side_effects=True, vmem_limit_bytes=60 * 1024 * 1024
        ),
        cost_estimate=pl.CostEstimate(
            flops=flops, bytes_accessed=64 * 1024 * 1024, transcendentals=0
        ),
    )(embedded, w_key, w_value, w_query)


def short_conv(ext, taps):
    values = ext.astype(jnp.float32)
    rows = values.shape[0] - 2
    return taps[0] * values[2:] + taps[1] * values[1 : rows + 1] + taps[2] * values[:rows]


def toeplitz(long_filter):
    tap_count = long_filter.shape[0]
    lag = (
        lax.broadcasted_iota(jnp.int32, (tap_count, 2 * tap_count), 0)
        + tap_count
        - lax.broadcasted_iota(jnp.int32, (tap_count, 2 * tap_count), 1)
    )
    hot = (lag[:, :, None] == lax.broadcasted_iota(jnp.int32, (1, 1, tap_count), 2)).astype(
        jnp.bfloat16
    )
    return jnp.einsum(
        "tsj,jg->gts",
        hot,
        long_filter.astype(jnp.bfloat16),
        preferred_element_type=jnp.float32,
    ).astype(jnp.bfloat16)


def long_conv(ext, matrix, row_count):
    groups, tap_count, _ = matrix.shape
    width = ext.shape[1]
    blocks = row_count // tap_count
    cut = ext.reshape(blocks + 1, tap_count, groups, width // groups)
    pair = jnp.concatenate([cut[:-1], cut[1:]], axis=1)
    out = jnp.einsum("gts,bsgc->btgc", matrix, pair, preferred_element_type=jnp.float32)
    return out.reshape(row_count, width)


def local(embedded, w_query, w_key, w_value, short_taps, long_filter, skip_gain):
    row_count = embedded.shape[0]
    tap_count = long_filter.shape[0]
    matrix = toeplitz(long_filter)
    key_rows, value_rows, query_rows = project(embedded, w_key, w_value, w_query)

    key_end, value_end = key_rows[-tap_count - 2 :], value_rows[-tap_count - 2 :]
    mixed_end = (short_conv(key_end, short_taps[1]) * short_conv(value_end, short_taps[2])).astype(
        jnp.bfloat16
    )
    edge = forward(
        jnp.concatenate([mixed_end, query_rows[-2:], key_rows[-2:], value_rows[-2:]], axis=0),
        "shard",
        1,
    )
    query_edge, key_edge, value_edge = [
        edge[tap_count + 2 * p : tap_count + 2 * p + 2] for p in range(3)
    ]
    query_short = short_conv(jnp.concatenate([query_edge, query_rows], axis=0), short_taps[0])
    key_short = short_conv(jnp.concatenate([key_edge, key_rows], axis=0), short_taps[1])
    value_short = short_conv(jnp.concatenate([value_edge, value_rows], axis=0), short_taps[2])
    mixed = (key_short * value_short).astype(jnp.bfloat16)
    long_out = long_conv(jnp.concatenate([edge[:tap_count], mixed], axis=0), matrix, row_count)
    return (query_short * (long_out + skip_gain * mixed.astype(jnp.float32))).astype(jnp.bfloat16)


def solution(mesh):
    in_specs = (
        P("shard", "ctx"),
        P("shard", "ctx"),
        P("shard", "ctx"),
        P("shard", "ctx"),
        P(None, None, "ctx"),
        P(None, "ctx"),
        P("ctx"),
    )
    return jax.shard_map(
        local, mesh=mesh, in_specs=in_specs, out_specs=P("shard", "ctx"), check_vma=False
    )
```

```python
import functools

import jax
import jax.numpy as jnp
from jax import lax
from jax.experimental import pallas as pl
from jax.experimental.pallas import tpu as pltpu
from jax.sharding import PartitionSpec as P

CHUNKS = 8
HALVES = 2
PIECES = 8
AHEAD = 3
TILE = 256
MESH = pl.DeviceIdType.MESH


def forward(value, axis, steps):
    count = lax.axis_size(axis)
    return lax.ppermute(value, axis, [(source, source + steps) for source in range(count - steps)])


def projection_kernel(
    names, embedded, w_key, w_value, w_query, out,
    wbuf, ebuf, gbuf, osend, orecv, acc,
    wy_sem, wc_sem, wo_sem, zs_sem, zr_sem, x_sem, o_sem, local_sem,
):
    shards, blocks = lax.axis_size(names[0]), lax.axis_size(names[1])
    per = shards // blocks
    groups = blocks // 2
    place, z = lax.axis_index(names[0]), lax.axis_index(names[1])
    core = place % per
    side = (place // per) % 2
    group = place // (2 * per)
    weights = (w_key, w_value, w_query)
    rows, wide = embedded.shape
    depth, width = w_key.shape
    piece = rows // CHUNKS
    half = rows // HALVES
    cut = depth // PIECES
    core_place = place + 1 - 2 * core
    side_place = place + per * (1 - 2 * side)

    def group_place(step):
        return lax.rem(group + step, groups) * 2 * per + side * per + core

    def remote(src, dst, send, recv, where):
        return pltpu.make_async_remote_copy(
            src_ref=src, dst_ref=dst, send_sem=send, recv_sem=recv,
            device_id=where, device_id_type=MESH,
        )

    def either(body, *conditions):
        flag = conditions[0]
        for other in conditions[1:]:
            flag = jnp.logical_and(flag, other)
        pl.when(flag)(body)

    barrier = pltpu.get_barrier_semaphore()
    partners = [core_place, side_place] + [group_place(j) for j in range(1, groups)]
    for partner in partners:
        pl.semaphore_signal(barrier, inc=1, device_id=(partner, z), device_id_type=MESH)

    @pl.when(z > 0)
    def _():
        pl.semaphore_signal(barrier, inc=1, device_id=(place, z - 1), device_id_type=MESH)

    @pl.when(z < blocks - 1)
    def _():
        pl.semaphore_signal(barrier, inc=1, device_id=(place, z + 1), device_id_type=MESH)

    ends = jnp.where(z > 0, 1, 0) + jnp.where(z < blocks - 1, 1, 0)
    pl.semaphore_wait(barrier, len(partners) + ends)

    def chunk(c):
        return pl.ds(c * piece, piece)

    def own_rows(k):
        return pl.ds(pl.multiple_of(core * depth + k * cut, 16), cut)

    pieces = [(p, j, k) for p in range(3) for j in range(1, groups) for k in range(PIECES)]

    def w_across(q):
        p, j, k = pieces[q]
        return remote(
            weights[p].at[pl.ds(k * cut, cut)], wbuf.at[p, j, own_rows(k)],
            wy_sem.at[0, q], wy_sem.at[1, q], (group_place(groups - j), z),
        )

    def w_core(q):
        p, j, k = pieces[q]
        ref = wbuf.at[p, j, own_rows(k)]
        return remote(ref, ref, wc_sem.at[0, q], wc_sem.at[1, q], (core_place, z))

    def w_own(p):
        mine = pl.ds(pl.multiple_of(core * depth, 16), depth)
        return remote(
            weights[p], wbuf.at[p, 0, mine], wo_sem.at[0, p], wo_sem.at[1, p], (core_place, z)
        )

    def w_here(p):
        mine = pl.ds(pl.multiple_of(core * depth, 16), depth)
        return pltpu.make_async_copy(weights[p], wbuf.at[p, 0, mine], local_sem.at[p])

    def up(c, r):
        src = embedded.at[chunk(c)] if r == 1 else ebuf.at[z - (r - 1), chunk(c)]
        return remote(
            src, ebuf.at[z - (r - 1), chunk(c)], zs_sem.at[0, c, r - 1], zr_sem.at[0, c, r - 1],
            (place, z + 1),
        )

    def down(c, r):
        src = embedded.at[chunk(c)] if r == 1 else ebuf.at[z + (r - 1), chunk(c)]
        return remote(
            src, ebuf.at[z + (r - 1), chunk(c)], zs_sem.at[1, c, r - 1], zr_sem.at[1, c, r - 1],
            (place, z - 1),
        )

    def across(c, f, src):
        return remote(
            src, gbuf.at[f // 2, chunk(c)], x_sem.at[0, c, f // 2], x_sem.at[1, c, f // 2],
            (side_place, z),
        )

    def own_embedded(c):
        either(lambda: up(c, 1).start(), z < blocks - 1)
        either(lambda: down(c, 1).start(), z > 0)
        either(lambda: across(c, z, embedded.at[chunk(c)]).start(), z % 2 != side)

    def step(c, r):
        @pl.when(z >= r)
        def _():
            f = z - r
            pltpu.make_async_copy(
                ebuf.at[f, chunk(c)], ebuf.at[f, chunk(c)], zr_sem.at[0, c, r - 1]
            ).wait()
            if r < blocks - 1:
                either(lambda: up(c, r + 1).start(), z < blocks - 1)
            either(lambda: across(c, f, ebuf.at[f, chunk(c)]).start(), f % 2 != side)

        @pl.when(z + r < blocks)
        def _():
            f = z + r
            pltpu.make_async_copy(
                ebuf.at[f, chunk(c)], ebuf.at[f, chunk(c)], zr_sem.at[1, c, r - 1]
            ).wait()
            if r < blocks - 1:
                either(lambda: down(c, r + 1).start(), z > 0)
            either(lambda: across(c, f, ebuf.at[f, chunk(c)]).start(), f % 2 != side)

    def product(p, h, lhs, store):
        at = pl.ds(h * half, half)

        def tile(n, carry):
            cols = pl.ds(pl.multiple_of(n * TILE, TILE), TILE)
            total = None
            for j in range(groups):
                term = jnp.dot(
                    lhs(j)[at, :], wbuf[p, j, :, cols], preferred_element_type=jnp.float32
                )
                total = term if total is None else total + term
            store(at, cols, total)
            return carry

        lax.fori_loop(0, width // TILE, tile, 0)

    def o_copy(p, h):
        at = pl.ds(h * half, half)
        return remote(
            osend.at[p, at], orecv.at[p, at], o_sem.at[0, p, h], o_sem.at[1, p, h], (side_place, z)
        )

    def give(p, h):
        def store(at, cols, total):
            osend[p, at, cols] = total.astype(jnp.bfloat16)

        product(p, h, lambda j: gbuf.at[lax.rem(group + j, groups)], store)
        o_copy(p, h).start()

    def keep(p, h):
        def store(at, cols, total):
            acc[p, at, cols] = total

        product(p, h, lambda j: ebuf.at[2 * lax.rem(group + j, groups) + side], store)

    def finish(p, h):
        at = pl.ds(h * half, half)
        o_copy(p, h).wait_recv()
        out[p, at, :] = (acc[p, at, :] + orecv[p, at, :].astype(jnp.float32)).astype(jnp.bfloat16)

    here = pltpu.make_async_copy(embedded, ebuf.at[z], local_sem.at[3])
    own_embedded(0)
    for q in range(min(AHEAD, len(pieces))):
        w_across(q).start()
    own_embedded(1)
    here.start()
    for p in range(3):
        w_here(p).start()
        w_own(p).start()
    here.wait()
    for p in range(3):
        w_here(p).wait()

    steps = CHUNKS * (blocks - 1)
    weight_ready, rows_ready = {}, {}
    done_pieces = 0
    waited_rows, waited_weights, finished = set(), set(), set()
    pending = [(p, h) for h in range(HALVES) for p in range(3)]
    kept = []

    def ready_rows(h):
        if h in waited_rows:
            return
        waited_rows.add(h)
        for c in range(h * CHUNKS // HALVES, (h + 1) * CHUNKS // HALVES):
            for g in range(groups):
                pltpu.make_async_copy(
                    gbuf.at[g, chunk(c)], gbuf.at[g, chunk(c)], x_sem.at[1, c, g]
                ).wait()

    def ready_weight(p):
        if p in waited_weights:
            return
        waited_weights.add(p)
        w_own(p).wait_recv()
        for q, (owner, _, _) in enumerate(pieces):
            if owner == p:
                w_core(q).wait_recv()

    t = 0
    for c in range(CHUNKS):
        for r in range(1, blocks):
            step(c, r)
            if r == 1 and c + 2 < CHUNKS:
                own_embedded(c + 2)
            while done_pieces < (t + 1) * len(pieces) // steps:
                w_across(done_pieces).wait_recv()
                w_core(done_pieces).start()
                if done_pieces + AHEAD < len(pieces):
                    w_across(done_pieces + AHEAD).start()
                done_pieces += 1
            chunks_in = c if r < blocks - 1 else c + 1
            last = t == steps - 1
            whole = [
                p for p in range(3)
                if done_pieces - (0 if last else 1) >= (p + 1) * (len(pieces) // 3)
            ]
            now = [
                (p, h) for p, h in pending
                if p in whole and (h + 1) * CHUNKS // HALVES <= (chunks_in if last else c)
            ]
            for p, h in now:
                pending.remove((p, h))
                ready_rows(h)
                ready_weight(p)
                give(p, h)
                if last:
                    kept.append((p, h))
                else:
                    keep(p, h)
            t += 1
    for p, h in kept:
        keep(p, h)
    for h in range(HALVES):
        for p in range(3):
            finish(p, h)

    for q in range(len(pieces)):
        w_across(q).wait_send()
        w_core(q).wait_send()
    for p in range(3):
        w_own(p).wait_send()
        for h in range(HALVES):
            o_copy(p, h).wait_send()
    for c in range(CHUNKS):
        for g in range(groups):
            pltpu.make_async_copy(
                gbuf.at[g, chunk(c)], gbuf.at[g, chunk(c)], x_sem.at[0, c, g]
            ).wait()
        for r in range(1, blocks):
            either(lambda: up(c, r).wait_send(), z < blocks - 1, z >= r - 1)
            either(lambda: down(c, r).wait_send(), z > 0, z + r - 1 < blocks)


def project(embedded, w_key, w_value, w_query):
    shards, blocks = lax.axis_size("shard"), lax.axis_size("ctx")
    groups = blocks // 2
    rows, wide = embedded.shape
    depth, width = w_key.shape
    pieces = 3 * (groups - 1) * PIECES
    bf16 = jnp.bfloat16
    dma = pltpu.SemaphoreType.DMA
    flops = 2 * 2 * rows * groups * wide * width * 3
    return pl.pallas_call(
        functools.partial(projection_kernel, ("shard", "ctx")),
        out_shape=jax.ShapeDtypeStruct((3, rows, width), bf16),
        in_specs=[pl.BlockSpec(memory_space=pl.ANY)] * 4,
        out_specs=pl.BlockSpec(memory_space=pltpu.VMEM),
        scratch_shapes=[
            pltpu.VMEM((3, groups, wide, width), bf16),
            pltpu.VMEM((blocks, rows, wide), bf16),
            pltpu.VMEM((groups, rows, wide), bf16),
            pltpu.VMEM((3, rows, width), bf16),
            pltpu.VMEM((3, rows, width), bf16),
            pltpu.VMEM((3, rows, width), jnp.float32),
            dma((2, pieces)),
            dma((2, pieces)),
            dma((2, 3)),
            dma((2, CHUNKS, blocks - 1)),
            dma((2, CHUNKS, blocks - 1)),
            dma((2, CHUNKS, groups)),
            dma((2, 3, HALVES)),
            dma((4,)),
        ],
        compiler_params=pltpu.CompilerParams(
            collective_id=0, has_side_effects=True, vmem_limit_bytes=60 * 1024 * 1024
        ),
        cost_estimate=pl.CostEstimate(
            flops=flops, bytes_accessed=64 * 1024 * 1024, transcendentals=0
        ),
    )(embedded, w_key, w_value, w_query)


def short_conv(ext, taps):
    values = ext.astype(jnp.float32)
    rows = values.shape[0] - 2
    return taps[0] * values[2:] + taps[1] * values[1 : rows + 1] + taps[2] * values[:rows]


def toeplitz(long_filter):
    tap_count = long_filter.shape[0]
    lag = (
        lax.broadcasted_iota(jnp.int32, (tap_count, 2 * tap_count), 0)
        + tap_count
        - lax.broadcasted_iota(jnp.int32, (tap_count, 2 * tap_count), 1)
    )
    hot = (lag[:, :, None] == lax.broadcasted_iota(jnp.int32, (1, 1, tap_count), 2)).astype(
        jnp.bfloat16
    )
    return jnp.einsum(
        "tsj,jg->gts",
        hot,
        long_filter.astype(jnp.bfloat16),
        preferred_element_type=jnp.float32,
    ).astype(jnp.bfloat16)


def long_conv(ext, matrix, row_count):
    groups, tap_count, _ = matrix.shape
    width = ext.shape[1]
    blocks = row_count // tap_count
    cut = ext.reshape(blocks + 1, tap_count, groups, width // groups)
    pair = jnp.concatenate([cut[:-1], cut[1:]], axis=1)
    out = jnp.einsum("gts,bsgc->btgc", matrix, pair, preferred_element_type=jnp.float32)
    return out.reshape(row_count, width)


def local(embedded, w_query, w_key, w_value, short_taps, long_filter, skip_gain):
    row_count = embedded.shape[0]
    tap_count = long_filter.shape[0]
    matrix = toeplitz(long_filter)
    key_rows, value_rows, query_rows = project(embedded, w_key, w_value, w_query)

    key_end, value_end = key_rows[-tap_count - 2 :], value_rows[-tap_count - 2 :]
    mixed_end = (short_conv(key_end, short_taps[1]) * short_conv(value_end, short_taps[2])).astype(
        jnp.bfloat16
    )
    edge = forward(
        jnp.concatenate([mixed_end, query_rows[-2:], key_rows[-2:], value_rows[-2:]], axis=0),
        "shard",
        1,
    )
    query_edge, key_edge, value_edge = [
        edge[tap_count + 2 * p : tap_count + 2 * p + 2] for p in range(3)
    ]
    query_short = short_conv(jnp.concatenate([query_edge, query_rows], axis=0), short_taps[0])
    key_short = short_conv(jnp.concatenate([key_edge, key_rows], axis=0), short_taps[1])
    value_short = short_conv(jnp.concatenate([value_edge, value_rows], axis=0), short_taps[2])
    mixed = (key_short * value_short).astype(jnp.bfloat16)
    long_out = long_conv(jnp.concatenate([edge[:tap_count], mixed], axis=0), matrix, row_count)
    return (query_short * (long_out + skip_gain * mixed.astype(jnp.float32))).astype(jnp.bfloat16)


def solution(mesh):
    in_specs = (
        P("shard", "ctx"),
        P("shard", "ctx"),
        P("shard", "ctx"),
        P("shard", "ctx"),
        P(None, None, "ctx"),
        P(None, "ctx"),
        P("ctx"),
    )
    return jax.shard_map(
        local, mesh=mesh, in_specs=in_specs, out_specs=P("shard", "ctx"), check_vma=False
    )
```
